256 devices in a mesh: mz: 128 (over y, x_lo, z, core), pix: 2 (over x_hi).
Axes of the slice: x: 4 (x_hi: 2, x_lo: 2; x = x_hi * 2 + x_lo), y: 4, z: 8, core: 2. Of those that a mesh axis runs over, the one named last changes fastest.
Arguments:
- residual: float32 [128, 128, 16384], P('pix', None, 'mz'), may hold values from -6 to 6
- tissue_mask: int32 [128, 128], P('pix'), may hold values 0 or 1
- peak_class: int32 [16384], P('mz'), may hold values from 0 to 3
- peak_taps: float32 [4, 384], replicated, may hold values from -0.3125 to 0.3125
- blur_taps: float32 [9, 9], replicated, may hold values from -0.625 to 0.625
Outputs:
- gradient: float32 [128, 128, 16384], P('pix', None, 'mz')
The draws below stay inside these ranges and needn't reach their ends.
All inputs are finite; a program needn't handle non-finite values. No bound on the sum of `tissue_mask` on one device may be relied on, other than what follows from the above.
Results may differ from the reference program's by a relative error of at most 0.0003.
Values sent between devices are 32-bit elements; how exact they have to be, the bound alone decides.
A program may use at most 128 MiB of HBM per device.

```python
import jax
import jax.numpy as jnp
from jax import lax

COLS = 128
BINS_DEV = 128
BAND = 384
CLASSES = 4
ROWS = 128
BINS = 16384


def place_ends(drawn, rng, least, largest):
    index_at = [jax.random.randint(jax.random.fold_in(rng, axis), (), 0, length) for axis, length in enumerate(drawn.shape)]
    widest = drawn.shape.index(max(drawn.shape))
    next_to = index_at[:widest] + [(index_at[widest] + 1) % drawn.shape[widest]] + index_at[widest + 1:]
    return drawn.at[tuple(index_at)].set(least).at[tuple(next_to)].set(largest)


def steps_of(stream_key, shape, cuts, low, high):
    def one(dim, shards_of):
        heights = jax.random.uniform(jax.random.fold_in(jax.random.fold_in(stream_key, 6), dim), (shards_of,), jnp.float32, low / len(cuts), high / len(cuts))
        return jnp.repeat(jnp.exp(heights), shape[dim] // shards_of).reshape((-1,) + (1,) * (len(shape) - dim - 1))

    loudness = one(*cuts[0])
    for cut in cuts[1:]:
        loudness = loudness * one(*cut)
    return loudness


def centred(key, extent, spread, bound, pieces=(), kind=jnp.bfloat16):
    factor_of = steps_of(key, extent, pieces, -0.22, 0.18) if pieces else 1.0
    drawn = jax.random.normal(key, extent, jnp.float32) * spread * factor_of
    return jnp.minimum(jnp.maximum(drawn, -bound), bound).astype(kind)


def setup_inputs(seed: int = 0) -> dict:
    key_list = jax.random.split(jax.random.key(seed), 6)
    residual = centred(key_list[0], (ROWS, COLS, BINS), 1.0, 6.0, ((0, 2), (2, 128)), jnp.float32)
    tissue_mask = place_ends((jax.random.randint(key_list[1], (ROWS, COLS), 0, 4) < 3).astype(jnp.int32), jax.random.fold_in(key_list[1], 1), 0, 1)
    peak_class = place_ends(jax.random.randint(key_list[2], (BINS,), 0, CLASSES), jax.random.fold_in(key_list[2], 1), 0, CLASSES - 1).astype(jnp.int32)
    peak_taps = centred(key_list[3], (CLASSES, BAND), BAND ** -0.5, 0.3125, (), jnp.float32)
    blur_taps = centred(key_list[4], (9, 9), 81 ** -0.5, 0.625, (), jnp.float32)
    return {"residual": residual, "tissue_mask": tissue_mask, "peak_class": peak_class, "peak_taps": peak_taps, "blur_taps": blur_taps}


def class_rows(classes, peak_taps):
    rows = jnp.zeros((classes.shape[0], peak_taps.shape[1]), jnp.float32)
    for level in range(peak_taps.shape[0]):
        rows = rows + jnp.where((classes == level)[:, None], peak_taps[level][None, :], jnp.float32(0.0))
    return rows


def band_matrix(kernel_rows, offsets):
    band = kernel_rows.shape[1]
    valid = (offsets >= 0) & (offsets < band)
    picked = jnp.take_along_axis(kernel_rows, jnp.clip(offsets, 0, band - 1).astype(jnp.int32), axis=1)
    return jnp.where(valid, picked, jnp.float32(0.0))


def reference(residual, tissue_mask, peak_class, peak_taps, blur_taps):
    rows, cols, bins = residual.shape
    half = peak_taps.shape[1] // 2
    width = BINS_DEV
    slabs = bins // width
    span = width + 2 * half
    masked = (residual * tissue_mask.astype(jnp.float32)[:, :, None]).reshape(rows * cols, bins)
    padded = jnp.pad(masked, ((0, 0), (half, half)))
    padded_classes = jnp.pad(peak_class, (half, half))
    kernel_all = class_rows(padded_classes, peak_taps)
    source = lax.broadcasted_iota(jnp.int32, (span, width), 0)
    target = lax.broadcasted_iota(jnp.int32, (span, width), 1)
    offsets = target - source + 2 * half

    def one_slab(index):
        start = (index * width).astype(jnp.int32)
        window = lax.dynamic_slice_in_dim(padded, start, span, 1)
        kernel_rows = lax.dynamic_slice_in_dim(kernel_all, start, span, 0)
        band = band_matrix(kernel_rows, offsets)
        return jnp.dot(window, band, precision=lax.Precision.HIGHEST, preferred_element_type=jnp.float32)

    stacked = lax.map(one_slab, jnp.arange(slabs, dtype=jnp.int32))
    spectral = jnp.transpose(stacked, (1, 0, 2)).reshape(rows, cols, slabs, width)
    spectral = jnp.transpose(spectral, (2, 0, 1, 3))

    def blur_slab(block):
        framed = jnp.pad(block, ((4, 4), (4, 4), (0, 0)))
        total = jnp.zeros(block.shape, jnp.float32)
        for tap_row in range(9):
            for tap_col in range(9):
                total = total + blur_taps[tap_row, tap_col] * framed[8 - tap_row:8 - tap_row + rows, 8 - tap_col:8 - tap_col + cols]
        return total

    blurred = lax.map(blur_slab, spectral)
    return jnp.transpose(blurred, (1, 2, 0, 3)).reshape(rows, cols, bins)
```

```python
import functools

import jax
import jax.numpy as jnp
from jax import lax
from jax.experimental import pallas as pl
from jax.experimental.pallas import tpu as pltpu
from jax.sharding import PartitionSpec as P

MESH = pl.DeviceIdType.MESH
F32 = jnp.float32
BF16 = jnp.bfloat16
WIDTH = 128
COLS = 128
STEP = 4
AHEAD = 3
FAR_AHEAD = 8
EDGE_AT = 14
LINE = 16


def split(values):
    high = values.astype(BF16)
    return high, (values - high.astype(F32)).astype(BF16)


def dot(a, b):
    return jnp.dot(a, b, preferred_element_type=F32)


def column(row):
    return jnp.broadcast_to(row, (WIDTH, row.shape[1])).T


def kernel(
    slabs, rows,
    x_ref, mask_hbm, class_hbm, taps_hbm, blur_hbm, out_ref,
    mask_ref, class_ref, taps_ref, blur_ref, own, far, near, beyond, half, packed, spectral, blur_high, blur_low,
    stack, band, half_high, half_low, edge_out, edge_in, classes,
    small_sem, own_sem, far_send, far_recv, near_send, near_recv, on_send, on_recv,
    half_send, half_recv, edge_sems, class_send, class_recv,
):
    m = lax.axis_index("mz")
    pix = lax.axis_index("pix")
    core = lax.rem(m, 2)
    side = 1 - 2 * core
    partner, next_chip, two_on, two_back = (m + side, m - side, m + 2 * side, m - 2 * side)
    inside = (m > 0) & (m < slabs - 1)
    late = (lax.rem(m, LINE) < 2) | (lax.rem(m, LINE) >= LINE - 2)
    sends_half = (two_on >= 0) & (two_on < slabs)
    chunks = rows // STEP
    size = STEP * COLS

    def base(c):
        return jnp.where(pix == 0, rows - STEP * (c + 1), STEP * c)

    def at(c):
        return pl.ds(base(c), STEP)

    def remote(src, dst, send, recv, to):
        return pltpu.make_async_remote_copy(
            src_ref=src, dst_ref=dst, send_sem=send, recv_sem=recv,
            device_id=to, device_id_type=MESH,
        )

    def load_own(c):
        return pltpu.make_async_copy(x_ref.at[at(c)], own.at[at(c)], own_sem.at[c])

    def to_far(c):
        return remote(x_ref.at[at(c)], far.at[at(c)], far_send.at[c], far_recv.at[c], (next_chip, pix))

    def to_near(c):
        return remote(x_ref.at[at(c)], near.at[at(c)], near_send.at[c], near_recv.at[c], (partner, pix))

    def pass_on(c):
        return remote(far.at[at(c)], beyond.at[at(c)], on_send.at[c], on_recv.at[c], (partner, pix))

    def to_half(c):
        return remote(packed.at[c], half.at[c], half_send.at[c], half_recv.at[c], (two_on, pix))

    def to_edge():
        return remote(edge_out, edge_in, edge_sems.at[0], edge_sems.at[1], (m, 1 - pix))

    def class_copy(src, slot, to):
        return remote(classes.at[src], classes.at[slot], class_send.at[slot], class_recv.at[slot], (to, pix))

    class_near = class_copy(0, 1, partner)
    class_far = class_copy(0, 2, next_chip)
    class_half = class_copy(0, 3, two_on)
    class_on = class_copy(2, 4, partner)

    barrier = pltpu.get_barrier_semaphore()
    pl.semaphore_signal(barrier, inc=1, device_id=(partner, pix), device_id_type=MESH)
    pl.semaphore_signal(barrier, inc=1, device_id=(m, 1 - pix), device_id_type=MESH)

    @pl.when(inside)
    def _():
        pl.semaphore_signal(barrier, inc=1, device_id=(next_chip, pix), device_id_type=MESH)
        pl.semaphore_signal(barrier, inc=1, device_id=(two_back, pix), device_id_type=MESH)

    def loop(count, body):
        lax.fori_loop(0, count, lambda i, carry: (body(i), carry)[1], 0)

    small = [
        pltpu.make_async_copy(src, dst, small_sem.at[i])
        for i, (src, dst) in enumerate(
            ((class_hbm, class_ref), (blur_hbm, blur_ref), (taps_hbm, taps_ref), (mask_hbm, mask_ref))
        )
    ]
    for copy in small:
        copy.start()
    loop(chunks, lambda c: load_own(c).start())
    small[0].wait()
    classes[0] = jnp.broadcast_to(class_ref[...], (8, WIDTH))
    pl.semaphore_wait(barrier, 2 + inside.astype(jnp.int32) + sends_half.astype(jnp.int32))

    @pl.when(inside)
    def _():
        class_far.start()
        loop(FAR_AHEAD, lambda c: to_far(c).start())

    class_near.start()

    @pl.when(sends_half)
    def _():
        class_half.start()

    low_lanes = lax.broadcasted_iota(jnp.int32, (size // 2, WIDTH), 1) < WIDTH // 2
    rolled_lanes = low_lanes == (core == 0)

    def pack(c):
        load_own(c).wait()
        to_near(c).start()
        pair = STEP // 2
        moved = own[pl.ds(base(c) + pair * core, pair)].reshape(size // 2, WIDTH)
        stays = own[pl.ds(base(c) + pair * (1 - core), pair)].reshape(size // 2, WIDTH)
        packed[c] = jnp.where(rolled_lanes, pltpu.roll(moved, WIDTH // 2, 1), stays)

        @pl.when(sends_half)
        def _():
            to_half(c).start()

    loop(AHEAD, pack)
    for copy in small[1:]:
        copy.wait()

    blur_high[...] = jnp.zeros_like(blur_high)
    blur_low[...] = jnp.zeros_like(blur_low)
    offset = (
        lax.broadcasted_iota(jnp.int32, (COLS, COLS), 0)
        - lax.broadcasted_iota(jnp.int32, (COLS, COLS), 1)
        + 4
    )
    for a in range(9):
        toeplitz = jnp.zeros((COLS, COLS), F32)
        for b in range(9):
            toeplitz = jnp.where(offset == b, blur_ref[a, b], toeplitz)
        high, low = split(toeplitz)
        for r in range(STEP):
            place = (slice(r * COLS, (r + 1) * COLS), slice((r + 8 - a) * COLS, (r + 9 - a) * COLS))
            blur_high[place] = high
            blur_low[place] = low

    taps = taps_ref.shape[1]
    for k in range(taps_ref.shape[0]):
        wide = jnp.concatenate(
            [jnp.broadcast_to(taps_ref[k : k + 1, :], (WIDTH, taps)), jnp.zeros((WIDTH, 5 * WIDTH - taps), F32)], axis=1
        )
        wide = pltpu.roll(wide, WIDTH // 2, 1, stride=1, stride_axis=0)
        for block in range(5):
            stack[k, block] = wide[:, block * WIDTH : (block + 1) * WIDTH]

    def weights(slot, block):
        level = column(classes[slot, 0:1, :])
        total = jnp.zeros((WIDTH, WIDTH), F32)
        for k in range(taps_ref.shape[0]):
            total = total + jnp.where(level == k, stack[k, block], F32(0.0))
        return total

    def keep(place, slot, block):
        high, low = split(weights(slot, block))
        band[place * WIDTH : (place + 1) * WIDTH, :WIDTH] = high
        band[place * WIDTH : (place + 1) * WIDTH, WIDTH:] = low

    @pl.when(inside)
    def _():
        class_far.wait_recv()
        class_half.wait_recv()

    @pl.when(jnp.logical_not(inside))
    def _():
        classes[2] = jnp.zeros_like(classes[2])
        classes[3] = jnp.zeros_like(classes[3])

    class_on.start()
    keep(0, 0, 2)
    class_near.wait_recv()
    keep(1, 1, 1 + 2 * core)
    keep(2, 2, 3 - 2 * core)
    outer = weights(3, 4 - 4 * core)
    other = pltpu.roll(outer, WIDTH // 2, 0)
    for place, value in ((0, jnp.where(core == 0, other, outer)), (1, jnp.where(core == 0, outer, other))):
        high, low = split(value)
        half_high[:, place * WIDTH : (place + 1) * WIDTH] = high
        half_low[:, place * WIDTH : (place + 1) * WIDTH] = low
    class_on.wait_recv()
    keep(3, 4, 4 * core)

    def keep_spectral(row, values):
        high, low = split(values)
        place = pl.ds(pl.multiple_of(row * COLS, size), size)
        spectral[place, :WIDTH] = high
        spectral[place, WIDTH:] = low

    keep_spectral(jnp.where(pix == 0, 0, rows + 4), jnp.zeros((size, WIDTH), F32))

    def banded(c, refs, first):
        rows_of = slice(first * WIDTH, (first + 2) * WIDTH)
        high, low = split(jnp.concatenate([ref[at(c)].reshape(size, WIDTH) for ref in refs], axis=1))
        both = dot(high, band[rows_of, :])
        return both[:, :WIDTH] + both[:, WIDTH:] + dot(low, band[rows_of, :WIDTH])

    def early_part(c):
        high, low = split(half[c])
        extra = dot(high, half_high[...]) + dot(high, half_low[...]) + dot(low, half_high[...])
        return banded(c, (own, near), 0) + jnp.concatenate([extra[:, :WIDTH], extra[:, WIDTH:]], axis=0)

    def late_part(c):
        return banded(c, (far, beyond), 2)

    def tissue(c):
        rows_of = [column(mask_ref[pl.ds(base(c) + r, 1), :].astype(F32)) for r in range(STEP)]
        return jnp.concatenate(rows_of, axis=0)

    def window(c, start, groups):
        lanes = pl.ds(pl.multiple_of(start * size, size), groups * size)
        place = pl.ds(pl.multiple_of(base(c) * COLS + start * size, size), groups * size)
        both = dot(blur_high[:, lanes], spectral[place, :])
        return both[:, :WIDTH] + both[:, WIDTH:] + dot(blur_low[:, lanes], spectral[place, :WIDTH])

    def keep_out(c, values):
        out_ref[at(c)] = values.reshape(STEP, COLS, WIDTH)

    def blur(c):
        keep_out(c, window(c, 0, 3))

    def arrive_near(c):
        to_near(c).wait_recv()

        @pl.when(inside)
        def _():
            to_half(c).wait_recv()

        @pl.when(jnp.logical_not(inside))
        def _():
            half[c] = jnp.zeros((size // 2, WIDTH), F32)

    def arrive_far(c):
        @pl.when(inside)
        def _():
            to_far(c).wait_recv()

        @pl.when(jnp.logical_not(inside))
        def _():
            far[at(c)] = jnp.zeros((STEP, COLS, WIDTH), F32)

        pass_on(c).start()

    def take_edge():
        to_edge().wait_recv()
        keep_spectral(jnp.where(pix == 0, rows + 4, 0), edge_in[...])
        blur(0)

    def step(c):
        @pl.when(inside & (c + FAR_AHEAD < chunks))
        def _():
            to_far(c + FAR_AHEAD).start()

        @pl.when(c + AHEAD < chunks)
        def _():
            pack(c + AHEAD)

        @pl.when(c >= 3)
        def _():
            blur(c - 2)

        @pl.when(jnp.logical_not(late) & (c == EDGE_AT))
        def _():
            take_edge()

        arrive_far(c)
        arrive_near(c)
        values = early_part(c)
        pass_on(c).wait_recv()
        values = (values + late_part(c)) * tissue(c)
        keep_spectral(base(c) + 4, values)

        @pl.when(c == 0)
        def _():
            edge_out[...] = values

        @pl.when(jnp.logical_not(late) & (c == 0))
        def _():
            to_edge().start()

    last = chunks - 1
    loop(last, step)

    blur(last - 2)
    keep_out(last - 1, window(last - 1, 1 - pix, 2))
    keep_out(last, window(last, 2 - 2 * pix, 1))
    arrive_far(last)

    @pl.when(late)
    def _():
        to_edge().start()

    arrive_near(last)
    values = early_part(last)
    cover = tissue(last)
    pass_on(last).wait_recv()
    keep_spectral(base(last) + 4, (values + late_part(last)) * cover)
    for c, start in ((last - 1, 2 * pix), (last, 1)):
        out_ref[at(c)] = out_ref[at(c)] + window(c, start, 1).reshape(STEP, COLS, WIDTH)

    @pl.when(late)
    def _():
        take_edge()

    to_edge().wait_send()
    class_near.wait_send()
    class_on.wait_send()

    @pl.when(inside)
    def _():
        class_far.wait_send()
        loop(chunks, lambda c: to_far(c).wait_send())

    @pl.when(sends_half)
    def _():
        class_half.wait_send()
        loop(chunks, lambda c: to_half(c).wait_send())

    def finish(c):
        to_near(c).wait_send()
        pass_on(c).wait_send()

    loop(chunks, finish)


def per_device(residual, tissue_mask, peak_class, peak_taps, blur_taps):
    rows, cols, width = residual.shape
    chunks = rows // STEP
    size = STEP * cols
    slabs = lax.axis_size("mz")
    block = (rows, cols, width)
    dma = pltpu.SemaphoreType.DMA
    return pl.pallas_call(
        functools.partial(kernel, slabs, rows),
        out_shape=jax.ShapeDtypeStruct(block, F32),
        in_specs=[pl.BlockSpec(memory_space=pltpu.HBM)] * 5,
        out_specs=pl.BlockSpec(memory_space=pltpu.VMEM),
        scratch_shapes=[
            pltpu.VMEM(tissue_mask.shape, jnp.int32),
            pltpu.VMEM((1, width), jnp.int32),
            pltpu.VMEM(peak_taps.shape, F32),
            pltpu.SMEM(blur_taps.shape, F32),
            pltpu.VMEM(block, F32),
            pltpu.VMEM(block, F32),
            pltpu.VMEM(block, F32),
            pltpu.VMEM(block, F32),
            pltpu.VMEM((chunks, size // 2, width), F32),
            pltpu.VMEM((chunks, size // 2, width), F32),
            pltpu.VMEM(((rows + 8) * cols, 2 * width), BF16),
            pltpu.VMEM((size, (STEP + 8) * cols), BF16),
            pltpu.VMEM((size, (STEP + 8) * cols), BF16),
            pltpu.VMEM((peak_taps.shape[0], 5, width, width), F32),
            pltpu.VMEM((4 * width, 2 * width), BF16),
            pltpu.VMEM((width, 2 * width), BF16),
            pltpu.VMEM((width, 2 * width), BF16),
            pltpu.VMEM((size, width), F32),
            pltpu.VMEM((size, width), F32),
            pltpu.VMEM((5, 8, width), jnp.int32),
            dma((4,)),
            dma((chunks,)),
            dma((chunks,)),
            dma((chunks,)),
            dma((chunks,)),
            dma((chunks,)),
            dma((chunks,)),
            dma((chunks,)),
            dma((chunks,)),
            dma((chunks,)),
            dma((2,)),
            dma((5,)),
            dma((5,)),
        ],
        compiler_params=pltpu.CompilerParams(
            collective_id=0, has_side_effects=True, vmem_limit_bytes=48 * 2**20
        ),
    )(residual, tissue_mask, peak_class.reshape(1, width), peak_taps, blur_taps)


def solution(mesh):
    in_specs = (P("pix", None, "mz"), P("pix", None), P("mz"), P(), P())
    out_specs = P("pix", None, "mz")
    return jax.shard_map(
        per_device, mesh=mesh, in_specs=in_specs, out_specs=out_specs, check_vma=False
    )
```

```python
import functools

import jax
import jax.numpy as jnp
from jax import lax
from jax.experimental import pallas as pl
from jax.experimental.pallas import tpu as pltpu
from jax.sharding import PartitionSpec as P

MESH = pl.DeviceIdType.MESH
F32 = jnp.float32
BF16 = jnp.bfloat16
WIDTH = 128
COLS = 128
CLASSES = 4
STEP = 4
AHEAD = 3
FAR_AHEAD = 4
RELAY_AT = 7
EDGE_AT = 14
LINE = 16


def split(values):
    high = values.astype(BF16)
    return high, (values - high.astype(F32)).astype(BF16)


def dot(a, b):
    return jnp.dot(a, b, preferred_element_type=F32)


def column(row):
    return jnp.broadcast_to(row, (WIDTH, row.shape[1])).T


def gather_small(mask_hbm, class_hbm, blur_hbm, taps_hbm, out_ref, mask_ref, class_ref, blur_ref, taps_ref, sems):
    pairs = ((mask_hbm, mask_ref), (class_hbm, class_ref), (blur_hbm, blur_ref), (taps_hbm, taps_ref))
    copies = [pltpu.make_async_copy(src, dst, sems.at[i]) for i, (src, dst) in enumerate(pairs)]
    for copy in copies:
        copy.start()
    for copy in copies:
        copy.wait()
    rows = mask_ref.shape[0]
    out_ref[:rows] = mask_ref[...].astype(F32)
    out_ref[rows : rows + 8] = jnp.broadcast_to(class_ref[...].astype(F32), (8, WIDTH))
    out_ref[rows + 8 : rows + 17, :9] = blur_ref[...]
    for i in range(3):
        out_ref[rows + 24 + 4 * i : rows + 28 + 4 * i] = taps_ref[:, i * WIDTH : (i + 1) * WIDTH]


def kernel(
    slabs, rows,
    x_ref, small_ref, out_ref, blur_ref, own, far, near, beyond, half, packed, spectral, blur_high, blur_low,
    stack, band, half_high, half_low, edge_out, edge_in, relay, classes,
    small_sem, own_sem, far_send, far_recv, near_send, near_recv, on_send, on_recv,
    half_send, half_recv, edge_sems, class_send, class_recv, ready,
):
    m = lax.axis_index("mz")
    pix = lax.axis_index("pix")
    core = lax.rem(m, 2)
    side = 1 - 2 * core
    partner, next_chip, two_on, two_back = (m + side, m - side, m + 2 * side, m - 2 * side)
    inside = (m > 0) & (m < slabs - 1)
    sends_half = (two_on >= 0) & (two_on < slabs)
    place_on_line = lax.rem(m, LINE)
    follows = (place_on_line < 2) & (m >= LINE)
    ends = place_on_line >= LINE - 2
    line_end = (place_on_line < 2) | ends
    relayed = follows | ends
    inward = jnp.where(place_on_line < 2, m + 2, m - 2)
    relays = ((place_on_line >= 2) & (place_on_line < 4) & (m >= LINE)) | (
        (place_on_line >= LINE - 4) & (place_on_line < LINE - 2)
    )
    relays_for = jnp.where(place_on_line < 4, m - 2, m + 2)
    calls_up = (place_on_line == LINE - 1) & (m < slabs - 1)
    far_later = follows & (core == 0)
    half_later = follows & (core == 1)
    chunks = rows // STEP
    size = STEP * COLS

    def base(c):
        return jnp.where(pix == 0, rows - STEP * (c + 1), STEP * c)

    def at(c):
        return pl.ds(base(c), STEP)

    def remote(src, dst, send, recv, to):
        return pltpu.make_async_remote_copy(
            src_ref=src, dst_ref=dst, send_sem=send, recv_sem=recv,
            device_id=to, device_id_type=MESH,
        )

    def load_own(c):
        return pltpu.make_async_copy(x_ref.at[at(c)], own.at[at(c)], own_sem.at[c])

    def to_far(c):
        return remote(x_ref.at[at(c)], far.at[at(c)], far_send.at[c], far_recv.at[c], (next_chip, pix))

    def to_near(c):
        return remote(x_ref.at[at(c)], near.at[at(c)], near_send.at[c], near_recv.at[c], (partner, pix))

    def pass_on(c):
        return remote(far.at[at(c)], beyond.at[at(c)], on_send.at[c], on_recv.at[c], (partner, pix))

    def to_half(c):
        return remote(packed.at[c], half.at[c], half_send.at[c], half_recv.at[c], (two_on, pix))

    def to_edge():
        return remote(edge_out, edge_in, edge_sems.at[0], edge_sems.at[1], (m, 1 - pix))

    first, second = pl.ds(0, size // 2), pl.ds(size // 2, size // 2)

    def to_edge_half():
        return remote(edge_out.at[second], edge_in.at[second], edge_sems.at[0], edge_sems.at[1], (m, 1 - pix))

    def to_relay():
        return remote(edge_out.at[first], relay, edge_sems.at[2], edge_sems.at[3], (inward, 1 - pix))

    def from_relay():
        return remote(relay, edge_in.at[first], edge_sems.at[4], edge_sems.at[5], (relays_for, pix))

    def class_copy(src, slot, to):
        return remote(classes.at[src], classes.at[slot], class_send.at[slot], class_recv.at[slot], (to, pix))

    class_near = class_copy(0, 1, partner)
    class_far = class_copy(0, 2, next_chip)
    class_half = class_copy(0, 3, two_on)
    class_on = class_copy(2, 4, partner)

    barrier = pltpu.get_barrier_semaphore()
    pl.semaphore_signal(barrier, inc=1, device_id=(partner, pix), device_id_type=MESH)
    pl.semaphore_signal(barrier, inc=1, device_id=(m, 1 - pix), device_id_type=MESH)

    def greet(when, to):
        @pl.when(when)
        def _():
            pl.semaphore_signal(barrier, inc=1, device_id=to, device_id_type=MESH)

    greet(inside & jnp.logical_not(calls_up), (next_chip, pix))
    greet(inside & jnp.logical_not(calls_up), (two_back, pix))
    greet(half_later, (two_on, pix))
    greet(relayed, (inward, pix))
    greet(relays, (relays_for, 1 - pix))

    def loop(count, body):
        lax.fori_loop(0, count, lambda i, carry: (body(i), carry)[1], 0)

    small_blur = pltpu.make_async_copy(small_ref.at[pl.ds(rows + 8, 16)], blur_ref, small_sem.at[0])
    small_blur.start()
    classes[0] = jnp.broadcast_to(small_ref[rows : rows + 1, :].astype(jnp.int32), (8, WIDTH))
    loop(chunks, lambda c: load_own(c).start())
    greetings = (inside, sends_half, calls_up, relays, ends)
    pl.semaphore_wait(barrier, 2 + sum(g.astype(jnp.int32) for g in greetings))

    @pl.when(calls_up)
    def _():
        pl.semaphore_signal(ready, inc=1, device_id=(next_chip, pix), device_id_type=MESH)
        pl.semaphore_signal(ready, inc=1, device_id=(two_back, pix), device_id_type=MESH)

    def first_far():
        class_far.start()
        loop(FAR_AHEAD, lambda c: to_far(c).start())

    @pl.when(inside & jnp.logical_not(far_later))
    def _():
        first_far()

    class_near.start()

    @pl.when(sends_half & jnp.logical_not(half_later))
    def _():
        class_half.start()

    low_lanes = lax.broadcasted_iota(jnp.int32, (size // 2, WIDTH), 1) < WIDTH // 2
    rolled_lanes = low_lanes == (core == 0)

    def pack(c, may_send):
        load_own(c).wait()
        to_near(c).start()
        pair = STEP // 2
        moved = own[pl.ds(base(c) + pair * core, pair)].reshape(size // 2, WIDTH)
        stays = own[pl.ds(base(c) + pair * (1 - core), pair)].reshape(size // 2, WIDTH)
        packed[c] = jnp.where(rolled_lanes, pltpu.roll(moved, WIDTH // 2, 1), stays)

        @pl.when(may_send)
        def _():
            to_half(c).start()

    loop(AHEAD, lambda c: pack(c, sends_half & jnp.logical_not(half_later)))

    @pl.when(follows)
    def _():
        pl.semaphore_wait(ready, 1)

    @pl.when(far_later)
    def _():
        first_far()

    @pl.when(half_later)
    def _():
        class_half.start()
        loop(AHEAD, lambda c: to_half(c).start())

    small_blur.wait()

    blur_high[...] = jnp.zeros_like(blur_high)
    blur_low[...] = jnp.zeros_like(blur_low)
    offset = (
        lax.broadcasted_iota(jnp.int32, (COLS, COLS), 0)
        - lax.broadcasted_iota(jnp.int32, (COLS, COLS), 1)
        + 4
    )
    for a in range(9):
        toeplitz = jnp.zeros((COLS, COLS), F32)
        for b in range(9):
            toeplitz = jnp.where(offset == b, blur_ref[a, b], toeplitz)
        high, low = split(toeplitz)
        for r in range(STEP):
            place = (slice(r * COLS, (r + 1) * COLS), slice((r + 8 - a) * COLS, (r + 9 - a) * COLS))
            blur_high[place] = high
            blur_low[place] = low

    for k in range(CLASSES):
        row = rows + 24 + k
        wide = jnp.concatenate(
            [jnp.broadcast_to(small_ref[row + 4 * i : row + 4 * i + 1, :], (WIDTH, WIDTH)) for i in range(3)]
            + [jnp.zeros((WIDTH, 2 * WIDTH), F32)],
            axis=1,
        )
        wide = pltpu.roll(wide, WIDTH // 2, 1, stride=1, stride_axis=0)
        for block in range(5):
            stack[k, block] = wide[:, block * WIDTH : (block + 1) * WIDTH]

    def weights(slot, block):
        level = column(classes[slot, 0:1, :])
        total = jnp.zeros((WIDTH, WIDTH), F32)
        for k in range(CLASSES):
            total = total + jnp.where(level == k, stack[k, block], F32(0.0))
        return total

    def keep(place, slot, block):
        high, low = split(weights(slot, block))
        band[place * WIDTH : (place + 1) * WIDTH, :WIDTH] = high
        band[place * WIDTH : (place + 1) * WIDTH, WIDTH:] = low

    @pl.when(inside)
    def _():
        class_far.wait_recv()
        class_half.wait_recv()

    @pl.when(jnp.logical_not(inside))
    def _():
        classes[2] = jnp.zeros_like(classes[2])
        classes[3] = jnp.zeros_like(classes[3])

    class_on.start()
    keep(0, 0, 2)
    class_near.wait_recv()
    keep(1, 1, 1 + 2 * core)
    keep(2, 2, 3 - 2 * core)
    outer = weights(3, 4 - 4 * core)
    other = pltpu.roll(outer, WIDTH // 2, 0)
    for place, value in ((0, jnp.where(core == 0, other, outer)), (1, jnp.where(core == 0, outer, other))):
        high, low = split(value)
        half_high[:, place * WIDTH : (place + 1) * WIDTH] = high
        half_low[:, place * WIDTH : (place + 1) * WIDTH] = low
    class_on.wait_recv()
    keep(3, 4, 4 * core)

    def keep_spectral(row, values):
        high, low = split(values)
        place = pl.ds(pl.multiple_of(row * COLS, size), size)
        spectral[place, :WIDTH] = high
        spectral[place, WIDTH:] = low

    keep_spectral(jnp.where(pix == 0, 0, rows + 4), jnp.zeros((size, WIDTH), F32))

    def banded(c, refs, first):
        rows_of = slice(first * WIDTH, (first + 2) * WIDTH)
        high, low = split(jnp.concatenate([ref[at(c)].reshape(size, WIDTH) for ref in refs], axis=1))
        both = dot(high, band[rows_of, :])
        return both[:, :WIDTH] + both[:, WIDTH:] + dot(low, band[rows_of, :WIDTH])

    def early_part(c):
        high, low = split(half[c])
        extra = dot(high, half_high[...]) + dot(high, half_low[...]) + dot(low, half_high[...])
        return banded(c, (own, near), 0) + jnp.concatenate([extra[:, :WIDTH], extra[:, WIDTH:]], axis=0)

    def late_part(c):
        return banded(c, (far, beyond), 2)

    def tissue(c):
        rows_of = [column(small_ref[pl.ds(base(c) + r, 1), :]) for r in range(STEP)]
        return jnp.concatenate(rows_of, axis=0)

    def window(c, start, groups):
        lanes = pl.ds(pl.multiple_of(start * size, size), groups * size)
        place = pl.ds(pl.multiple_of(base(c) * COLS + start * size, size), groups * size)
        both = dot(blur_high[:, lanes], spectral[place, :])
        return both[:, :WIDTH] + both[:, WIDTH:] + dot(blur_low[:, lanes], spectral[place, :WIDTH])

    def keep_out(c, values):
        out_ref[at(c)] = values.reshape(STEP, COLS, WIDTH)

    def blur(c):
        keep_out(c, window(c, 0, 3))

    def arrive_near(c):
        to_near(c).wait_recv()

        @pl.when(inside)
        def _():
            to_half(c).wait_recv()

        @pl.when(jnp.logical_not(inside))
        def _():
            half[c] = jnp.zeros((size // 2, WIDTH), F32)

    def arrive_far(c):
        @pl.when(inside)
        def _():
            to_far(c).wait_recv()

        @pl.when(jnp.logical_not(inside))
        def _():
            far[at(c)] = jnp.zeros((STEP, COLS, WIDTH), F32)

        pass_on(c).start()

    def keep_edge():
        keep_spectral(jnp.where(pix == 0, rows + 4, 0), edge_in[...])

    def add_out(c, values):
        out_ref[at(c)] = out_ref[at(c)] + values.reshape(STEP, COLS, WIDTH)

    def step(c):
        @pl.when(inside & (c + FAR_AHEAD < chunks))
        def _():
            to_far(c + FAR_AHEAD).start()

        @pl.when(c + AHEAD < chunks)
        def _():
            pack(c + AHEAD, sends_half)

        @pl.when(c >= 3)
        def _():
            blur(c - 2)

        @pl.when(relays & (c == RELAY_AT))
        def _():
            to_relay().wait_recv()
            from_relay().start()

        @pl.when(jnp.logical_not(line_end) & (c == EDGE_AT))
        def _():
            to_edge().wait_recv()
            keep_edge()
            blur(0)

        arrive_far(c)
        arrive_near(c)
        values = early_part(c)
        pass_on(c).wait_recv()
        values = (values + late_part(c)) * tissue(c)
        keep_spectral(base(c) + 4, values)

        @pl.when(c == 0)
        def _():
            edge_out[...] = values

        @pl.when(relayed & (c == 0))
        def _():
            to_relay().start()

        @pl.when(jnp.logical_not(line_end) & (c == 0))
        def _():
            to_edge().start()

    last = chunks - 1
    loop(last, step)

    blur(last - 2)
    keep_out(last - 1, window(last - 1, 1 - pix, 2))
    keep_out(last, window(last, 2 - 2 * pix, 1))

    @pl.when(line_end)
    def _():
        keep_out(0, window(0, pix, 2))

    arrive_far(last)

    @pl.when(relayed)
    def _():
        to_edge_half().start()

    @pl.when(line_end & jnp.logical_not(relayed))
    def _():
        to_edge().start()

    arrive_near(last)
    values = early_part(last)
    cover = tissue(last)
    pass_on(last).wait_recv()
    keep_spectral(base(last) + 4, (values + late_part(last)) * cover)
    for c, start in ((last - 1, 2 * pix), (last, 1)):
        add_out(c, window(c, start, 1))

    @pl.when(relayed)
    def _():
        from_relay().wait_recv()
        to_edge_half().wait()
        to_relay().wait_send()

    @pl.when(line_end & jnp.logical_not(relayed))
    def _():
        to_edge().wait()

    @pl.when(line_end)
    def _():
        keep_edge()
        add_out(0, window(0, 2 - 2 * pix, 1))

    @pl.when(jnp.logical_not(line_end))
    def _():
        to_edge().wait_send()

    @pl.when(relays)
    def _():
        from_relay().wait_send()

    class_near.wait_send()
    class_on.wait_send()

    @pl.when(inside)
    def _():
        class_far.wait_send()
        loop(chunks, lambda c: to_far(c).wait_send())

    @pl.when(sends_half)
    def _():
        class_half.wait_send()
        loop(chunks, lambda c: to_half(c).wait_send())

    def finish(c):
        to_near(c).wait_send()
        pass_on(c).wait_send()

    loop(chunks, finish)


def per_device(residual, tissue_mask, peak_class, peak_taps, blur_taps):
    rows, cols, width = residual.shape
    chunks = rows // STEP
    size = STEP * cols
    slabs = lax.axis_size("mz")
    block = (rows, cols, width)
    dma = pltpu.SemaphoreType.DMA
    small = pl.pallas_call(
        gather_small,
        out_shape=jax.ShapeDtypeStruct((rows + 40, width), F32),
        in_specs=[pl.BlockSpec(memory_space=pl.ANY)] * 4,
        out_specs=pl.BlockSpec(memory_space=pltpu.VMEM),
        scratch_shapes=[
            pltpu.VMEM(tissue_mask.shape, jnp.int32),
            pltpu.VMEM((1, width), jnp.int32),
            pltpu.VMEM(blur_taps.shape, F32),
            pltpu.VMEM(peak_taps.shape, F32),
            dma((4,)),
        ],
        compiler_params=pltpu.CompilerParams(vmem_limit_bytes=60 * 2**20),
    )(tissue_mask, peak_class.reshape(1, width), blur_taps, peak_taps)
    return pl.pallas_call(
        functools.partial(kernel, slabs, rows),
        out_shape=jax.ShapeDtypeStruct(block, F32),
        in_specs=[pl.BlockSpec(memory_space=pl.ANY), pl.BlockSpec(memory_space=pltpu.VMEM)],
        out_specs=pl.BlockSpec(memory_space=pltpu.VMEM),
        scratch_shapes=[
            pltpu.SMEM((16, width), F32),
            pltpu.VMEM(block, F32),
            pltpu.VMEM(block, F32),
            pltpu.VMEM(block, F32),
            pltpu.VMEM(block, F32),
            pltpu.VMEM((chunks, size // 2, width), F32),
            pltpu.VMEM((chunks, size // 2, width), F32),
            pltpu.VMEM(((rows + 8) * cols, 2 * width), BF16),
            pltpu.VMEM((size, (STEP + 8) * cols), BF16),
            pltpu.VMEM((size, (STEP + 8) * cols), BF16),
            pltpu.VMEM((CLASSES, 5, width, width), F32),
            pltpu.VMEM((4 * width, 2 * width), BF16),
            pltpu.VMEM((width, 2 * width), BF16),
            pltpu.VMEM((width, 2 * width), BF16),
            pltpu.VMEM((size, width), F32),
            pltpu.VMEM((size, width), F32),
            pltpu.VMEM((size // 2, width), F32),
            pltpu.VMEM((5, 8, width), jnp.int32),
            dma((2,)),
            dma((chunks,)),
            dma((chunks,)),
            dma((chunks,)),
            dma((chunks,)),
            dma((chunks,)),
            dma((chunks,)),
            dma((chunks,)),
            dma((chunks,)),
            dma((chunks,)),
            dma((6,)),
            dma((5,)),
            dma((5,)),
            pltpu.SemaphoreType.REGULAR,
        ],
        compiler_params=pltpu.CompilerParams(
            collective_id=0, has_side_effects=True, vmem_limit_bytes=48 * 2**20
        ),
    )(residual, small)


def solution(mesh):
    in_specs = (P("pix", None, "mz"), P("pix", None), P("mz"), P(), P())
    out_specs = P("pix", None, "mz")
    return jax.shard_map(
        per_device, mesh=mesh, in_specs=in_specs, out_specs=out_specs, check_vma=False
    )
```

```python
import functools

import jax
import jax.numpy as jnp
from jax import lax
from jax.experimental import pallas as pl
from jax.experimental.pallas import tpu as pltpu
from jax.sharding import PartitionSpec as P

MESH = pl.DeviceIdType.MESH
F32 = jnp.float32
BF16 = jnp.bfloat16
WIDTH = 128
COLS = 128
CLASSES = 4
STEP = 4
ROOM = 32768
AHEAD = 3
FAR_AHEAD = 8
RELAYED = 2
RELAY_AT = 10
EDGE_AT = 14
LINE = 16


def split(values):
    high = values.astype(BF16)
    return high, (values - high.astype(F32)).astype(BF16)


def dot(a, b):
    return jnp.dot(a, b, preferred_element_type=F32)


def column(row):
    return jnp.broadcast_to(row, (WIDTH, row.shape[1])).T


def gather_small(mask_hbm, class_hbm, blur_hbm, taps_hbm, out_hbm, out_ref, mask_ref, class_ref, blur_ref, taps_ref, sems):
    pairs = ((mask_hbm, mask_ref), (class_hbm, class_ref), (blur_hbm, blur_ref), (taps_hbm, taps_ref))
    copies = [pltpu.make_async_copy(src, dst, sems.at[i]) for i, (src, dst) in enumerate(pairs)]
    for copy in copies:
        copy.start()
    for copy in copies:
        copy.wait()
    rows = mask_ref.shape[0]
    out_ref[:rows] = mask_ref[...].astype(F32)
    out_ref[rows : rows + 8] = jnp.broadcast_to(class_ref[...].astype(F32), (8, WIDTH))
    out_ref[rows + 8 : rows + 17, :9] = blur_ref[...]
    for i in range(3):
        out_ref[rows + 24 + 4 * i : rows + 28 + 4 * i] = taps_ref[:, i * WIDTH : (i + 1) * WIDTH]
    back = pltpu.make_async_copy(out_ref, out_hbm.at[pl.ds(0, out_ref.shape[0])], sems.at[4])
    back.start()
    back.wait()


def kernel(
    slabs, rows,
    x_ref, small_hbm, out_ref, small_ref, blur_ref, own, far, near, beyond, half, packed, spectral, blur_high, blur_low,
    stack, band, half_high, half_low, edge_out, edge_in, relay, classes,
    small_sem, own_sem, far_send, far_recv, near_send, near_recv, on_send, on_recv,
    half_send, half_recv, edge_sems, class_send, class_recv, ready,
):
    m = lax.axis_index("mz")
    pix = lax.axis_index("pix")
    core = lax.rem(m, 2)
    side = 1 - 2 * core
    partner, next_chip, two_on, two_back = (m + side, m - side, m + 2 * side, m - 2 * side)
    inside = (m > 0) & (m < slabs - 1)
    sends_half = (two_on >= 0) & (two_on < slabs)
    place_on_line = lax.rem(m, LINE)
    follows = (place_on_line < 2) & (m >= LINE)
    ends = place_on_line >= LINE - 2
    line_end = (place_on_line < 2) | ends
    relayed = follows | ends
    inward = jnp.where(place_on_line < 2, m + 2, m - 2)
    relays = ((place_on_line >= 2) & (place_on_line < 4) & (m >= LINE)) | (
        (place_on_line >= LINE - 4) & (place_on_line < LINE - 2)
    )
    relays_for = jnp.where(place_on_line < 4, m - 2, m + 2)
    calls_up = (place_on_line == LINE - 1) & (m < slabs - 1)
    far_later = follows & (core == 0)
    half_later = follows & (core == 1)
    chunks = rows // STEP
    size = STEP * COLS

    def base(c):
        return jnp.where(pix == 0, rows - STEP * (c + 1), STEP * c)

    def at(c):
        return pl.ds(base(c), STEP)

    def remote(src, dst, send, recv, to):
        return pltpu.make_async_remote_copy(
            src_ref=src, dst_ref=dst, send_sem=send, recv_sem=recv,
            device_id=to, device_id_type=MESH,
        )

    def load_own(c):
        return pltpu.make_async_copy(x_ref.at[at(c)], own.at[at(c)], own_sem.at[c])

    def to_far(c):
        return remote(x_ref.at[at(c)], far.at[at(c)], far_send.at[c], far_recv.at[c], (next_chip, pix))

    def to_near(c):
        return remote(x_ref.at[at(c)], near.at[at(c)], near_send.at[c], near_recv.at[c], (partner, pix))

    def pass_on(c):
        return remote(far.at[at(c)], beyond.at[at(c)], on_send.at[c], on_recv.at[c], (partner, pix))

    def to_half(c):
        return remote(packed.at[c], half.at[c], half_send.at[c], half_recv.at[c], (two_on, pix))

    def to_edge():
        return remote(edge_out, edge_in, edge_sems.at[0], edge_sems.at[1], (m, 1 - pix))

    first, second = pl.ds(0, RELAYED * COLS), pl.ds(RELAYED * COLS, size - RELAYED * COLS)

    def to_edge_rest():
        return remote(edge_out.at[second], edge_in.at[second], edge_sems.at[0], edge_sems.at[1], (m, 1 - pix))

    def to_relay():
        return remote(edge_out.at[first], relay, edge_sems.at[2], edge_sems.at[3], (inward, 1 - pix))

    def from_relay():
        return remote(relay, edge_in.at[first], edge_sems.at[4], edge_sems.at[5], (relays_for, pix))

    def class_copy(src, slot, to):
        return remote(classes.at[src], classes.at[slot], class_send.at[slot], class_recv.at[slot], (to, pix))

    class_near = class_copy(0, 1, partner)
    class_far = class_copy(0, 2, next_chip)
    class_half = class_copy(0, 3, two_on)
    class_on = class_copy(2, 4, partner)

    barrier = pltpu.get_barrier_semaphore()
    pl.semaphore_signal(barrier, inc=1, device_id=(partner, pix), device_id_type=MESH)
    pl.semaphore_signal(barrier, inc=1, device_id=(m, 1 - pix), device_id_type=MESH)

    def greet(when, to):
        @pl.when(when)
        def _():
            pl.semaphore_signal(barrier, inc=1, device_id=to, device_id_type=MESH)

    greet(inside & jnp.logical_not(calls_up), (next_chip, pix))
    greet(inside & jnp.logical_not(calls_up), (two_back, pix))
    greet(half_later, (two_on, pix))
    greet(relayed, (inward, pix))
    greet(relays, (relays_for, 1 - pix))

    def loop(count, body):
        lax.fori_loop(0, count, lambda i, carry: (body(i), carry)[1], 0)

    small = pltpu.make_async_copy(small_hbm.at[pl.ds(0, rows + 40)], small_ref, small_sem.at[0])
    small_blur = pltpu.make_async_copy(small_hbm.at[pl.ds(rows + 8, 16)], blur_ref, small_sem.at[1])
    small.start()
    small_blur.start()

    greetings = (inside, sends_half, calls_up, relays, ends)
    pl.semaphore_wait(barrier, 2 + sum(g.astype(jnp.int32) for g in greetings))

    @pl.when(calls_up)
    def _():
        pl.semaphore_signal(ready, inc=1, device_id=(next_chip, pix), device_id_type=MESH)
        pl.semaphore_signal(ready, inc=1, device_id=(two_back, pix), device_id_type=MESH)

    @pl.when(inside & jnp.logical_not(far_later))
    def _():
        to_far(0).start()

    small.wait()
    classes[0] = jnp.broadcast_to(small_ref[rows : rows + 1, :].astype(jnp.int32), (8, WIDTH))

    def rest_of_far():
        class_far.start()
        lax.fori_loop(1, FAR_AHEAD, lambda c, carry: (to_far(c).start(), carry)[1], 0)

    @pl.when(inside & jnp.logical_not(far_later))
    def _():
        rest_of_far()

    class_near.start()
    loop(chunks, lambda c: load_own(c).start())

    @pl.when(sends_half & jnp.logical_not(half_later))
    def _():
        class_half.start()

    low_lanes = lax.broadcasted_iota(jnp.int32, (size // 2, WIDTH), 1) < WIDTH // 2
    rolled_lanes = low_lanes == (core == 0)

    def pack(c, may_send):
        load_own(c).wait()
        to_near(c).start()
        pair = STEP // 2
        moved = own[pl.ds(base(c) + pair * core, pair)].reshape(size // 2, WIDTH)
        stays = own[pl.ds(base(c) + pair * (1 - core), pair)].reshape(size // 2, WIDTH)
        packed[c] = jnp.where(rolled_lanes, pltpu.roll(moved, WIDTH // 2, 1), stays)

        @pl.when(may_send)
        def _():
            to_half(c).start()

    loop(AHEAD, lambda c: pack(c, sends_half & jnp.logical_not(half_later)))

    @pl.when(follows)
    def _():
        pl.semaphore_wait(ready, 1)

    @pl.when(far_later)
    def _():
        to_far(0).start()
        rest_of_far()

    @pl.when(half_later)
    def _():
        class_half.start()
        loop(AHEAD, lambda c: to_half(c).start())

    small_blur.wait()

    blur_high[...] = jnp.zeros_like(blur_high)
    blur_low[...] = jnp.zeros_like(blur_low)
    offset = (
        lax.broadcasted_iota(jnp.int32, (COLS, COLS), 0)
        - lax.broadcasted_iota(jnp.int32, (COLS, COLS), 1)
        + 4
    )
    for a in range(9):
        toeplitz = jnp.zeros((COLS, COLS), F32)
        for b in range(9):
            toeplitz = jnp.where(offset == b, blur_ref[a, b], toeplitz)
        high, low = split(toeplitz)
        for r in range(STEP):
            place = (slice(r * COLS, (r + 1) * COLS), slice((r + 8 - a) * COLS, (r + 9 - a) * COLS))
            blur_high[place] = high
            blur_low[place] = low

    for k in range(CLASSES):
        row = rows + 24 + k
        wide = jnp.concatenate(
            [jnp.broadcast_to(small_ref[row + 4 * i : row + 4 * i + 1, :], (WIDTH, WIDTH)) for i in range(3)]
            + [jnp.zeros((WIDTH, 2 * WIDTH), F32)],
            axis=1,
        )
        wide = pltpu.roll(wide, WIDTH // 2, 1, stride=1, stride_axis=0)
        for block in range(5):
            stack[k, block] = wide[:, block * WIDTH : (block + 1) * WIDTH]

    def weights(slot, block):
        level = column(classes[slot, 0:1, :])
        total = jnp.zeros((WIDTH, WIDTH), F32)
        for k in range(CLASSES):
            total = total + jnp.where(level == k, stack[k, block], F32(0.0))
        return total

    def keep(place, slot, block):
        high, low = split(weights(slot, block))
        band[place * WIDTH : (place + 1) * WIDTH, :WIDTH] = high
        band[place * WIDTH : (place + 1) * WIDTH, WIDTH:] = low

    @pl.when(inside)
    def _():
        class_far.wait_recv()
        class_half.wait_recv()

    @pl.when(jnp.logical_not(inside))
    def _():
        classes[2] = jnp.zeros_like(classes[2])
        classes[3] = jnp.zeros_like(classes[3])

    class_on.start()
    keep(0, 0, 2)
    class_near.wait_recv()
    keep(1, 1, 1 + 2 * core)
    keep(2, 2, 3 - 2 * core)
    outer = weights(3, 4 - 4 * core)
    other = pltpu.roll(outer, WIDTH // 2, 0)
    for place, value in ((0, jnp.where(core == 0, other, outer)), (1, jnp.where(core == 0, outer, other))):
        high, low = split(value)
        half_high[:, place * WIDTH : (place + 1) * WIDTH] = high
        half_low[:, place * WIDTH : (place + 1) * WIDTH] = low
    class_on.wait_recv()
    keep(3, 4, 4 * core)

    def keep_spectral(row, values):
        high, low = split(values)
        place = pl.ds(pl.multiple_of(row * COLS, size), size)
        spectral[place, :WIDTH] = high
        spectral[place, WIDTH:] = low

    keep_spectral(jnp.where(pix == 0, 0, rows + 4), jnp.zeros((size, WIDTH), F32))

    def banded(c, refs, first):
        rows_of = slice(first * WIDTH, (first + 2) * WIDTH)
        high, low = split(jnp.concatenate([ref[at(c)].reshape(size, WIDTH) for ref in refs], axis=1))
        both = dot(high, band[rows_of, :])
        return both[:, :WIDTH] + both[:, WIDTH:] + dot(low, band[rows_of, :WIDTH])

    def early_part(c):
        high, low = split(half[c])
        extra = dot(high, half_high[...]) + dot(high, half_low[...]) + dot(low, half_high[...])
        return banded(c, (own, near), 0) + jnp.concatenate([extra[:, :WIDTH], extra[:, WIDTH:]], axis=0)

    def late_part(c):
        return banded(c, (far, beyond), 2)

    def tissue(c):
        rows_of = [column(small_ref[pl.ds(base(c) + r, 1), :]) for r in range(STEP)]
        return jnp.concatenate(rows_of, axis=0)

    def window(c, start, groups):
        lanes = pl.ds(pl.multiple_of(start * size, size), groups * size)
        place = pl.ds(pl.multiple_of(base(c) * COLS + start * size, size), groups * size)
        both = dot(blur_high[:, lanes], spectral[place, :])
        return both[:, :WIDTH] + both[:, WIDTH:] + dot(blur_low[:, lanes], spectral[place, :WIDTH])

    def keep_out(c, values):
        out_ref[at(c)] = values.reshape(STEP, COLS, WIDTH)

    def blur(c):
        keep_out(c, window(c, 0, 3))

    def arrive_near(c):
        to_near(c).wait_recv()

        @pl.when(inside)
        def _():
            to_half(c).wait_recv()

        @pl.when(jnp.logical_not(inside))
        def _():
            half[c] = jnp.zeros((size // 2, WIDTH), F32)

    def arrive_far(c):
        @pl.when(inside)
        def _():
            to_far(c).wait_recv()

        @pl.when(jnp.logical_not(inside))
        def _():
            far[at(c)] = jnp.zeros((STEP, COLS, WIDTH), F32)

        pass_on(c).start()

    def keep_edge():
        keep_spectral(jnp.where(pix == 0, rows + 4, 0), edge_in[...])

    def add_out(c, values):
        out_ref[at(c)] = out_ref[at(c)] + values.reshape(STEP, COLS, WIDTH)

    def step(c):
        @pl.when(inside & (c + FAR_AHEAD < chunks))
        def _():
            to_far(c + FAR_AHEAD).start()

        @pl.when(c + AHEAD < chunks)
        def _():
            pack(c + AHEAD, sends_half)

        @pl.when(c >= 3)
        def _():
            blur(c - 2)

        @pl.when(relays & (c == RELAY_AT))
        def _():
            to_relay().wait_recv()
            from_relay().start()

        @pl.when(jnp.logical_not(line_end) & (c == EDGE_AT))
        def _():
            to_edge().wait_recv()
            keep_edge()
            blur(0)

        arrive_far(c)
        arrive_near(c)
        values = early_part(c)
        pass_on(c).wait_recv()
        values = (values + late_part(c)) * tissue(c)
        keep_spectral(base(c) + 4, values)

        @pl.when(c == 0)
        def _():
            edge_out[...] = values

        @pl.when(relayed & (c == 0))
        def _():
            to_relay().start()

        @pl.when(jnp.logical_not(line_end) & (c == 0))
        def _():
            to_edge().start()

    last = chunks - 1
    loop(last, step)

    blur(last - 2)
    keep_out(last - 1, window(last - 1, 1 - pix, 2))
    keep_out(last, window(last, 2 - 2 * pix, 1))

    @pl.when(line_end)
    def _():
        keep_out(0, window(0, pix, 2))

    arrive_far(last)

    @pl.when(relayed)
    def _():
        to_edge_rest().start()

    @pl.when(line_end & jnp.logical_not(relayed))
    def _():
        to_edge().start()

    arrive_near(last)
    values = early_part(last)
    cover = tissue(last)
    pass_on(last).wait_recv()
    keep_spectral(base(last) + 4, (values + late_part(last)) * cover)
    for c, start in ((last - 1, 2 * pix), (last, 1)):
        add_out(c, window(c, start, 1))

    @pl.when(relayed)
    def _():
        from_relay().wait_recv()
        to_edge_rest().wait()
        to_relay().wait_send()

    @pl.when(line_end & jnp.logical_not(relayed))
    def _():
        to_edge().wait()

    @pl.when(line_end)
    def _():
        keep_edge()
        add_out(0, window(0, 2 - 2 * pix, 1))

    @pl.when(jnp.logical_not(line_end))
    def _():
        to_edge().wait_send()

    @pl.when(relays)
    def _():
        from_relay().wait_send()

    class_near.wait_send()
    class_on.wait_send()

    @pl.when(inside)
    def _():
        class_far.wait_send()
        loop(chunks, lambda c: to_far(c).wait_send())

    @pl.when(sends_half)
    def _():
        class_half.wait_send()
        loop(chunks, lambda c: to_half(c).wait_send())

    def finish(c):
        to_near(c).wait_send()
        pass_on(c).wait_send()

    loop(chunks, finish)


def per_device(residual, tissue_mask, peak_class, peak_taps, blur_taps):
    rows, cols, width = residual.shape
    chunks = rows // STEP
    size = STEP * cols
    slabs = lax.axis_size("mz")
    block = (rows, cols, width)
    dma = pltpu.SemaphoreType.DMA
    small = pl.pallas_call(
        gather_small,
        out_shape=jax.ShapeDtypeStruct((ROOM, width), F32),
        in_specs=[pl.BlockSpec(memory_space=pl.ANY)] * 4,
        out_specs=pl.BlockSpec(memory_space=pl.ANY),
        scratch_shapes=[
            pltpu.VMEM((rows + 40, width), F32),
            pltpu.VMEM(tissue_mask.shape, jnp.int32),
            pltpu.VMEM((1, width), jnp.int32),
            pltpu.VMEM(blur_taps.shape, F32),
            pltpu.VMEM(peak_taps.shape, F32),
            dma((5,)),
        ],
        compiler_params=pltpu.CompilerParams(vmem_limit_bytes=60 * 2**20),
    )(tissue_mask, peak_class.reshape(1, width), blur_taps, peak_taps)
    return pl.pallas_call(
        functools.partial(kernel, slabs, rows),
        out_shape=jax.ShapeDtypeStruct(block, F32),
        in_specs=[pl.BlockSpec(memory_space=pl.ANY)] * 2,
        out_specs=pl.BlockSpec(memory_space=pltpu.VMEM),
        scratch_shapes=[
            pltpu.VMEM((rows + 40, width), F32),
            pltpu.SMEM((16, width), F32),
            pltpu.VMEM(block, F32),
            pltpu.VMEM(block, F32),
            pltpu.VMEM(block, F32),
            pltpu.VMEM(block, F32),
            pltpu.VMEM((chunks, size // 2, width), F32),
            pltpu.VMEM((chunks, size // 2, width), F32),
            pltpu.VMEM(((rows + 8) * cols, 2 * width), BF16),
            pltpu.VMEM((size, (STEP + 8) * cols), BF16),
            pltpu.VMEM((size, (STEP + 8) * cols), BF16),
            pltpu.VMEM((CLASSES, 5, width, width), F32),
            pltpu.VMEM((4 * width, 2 * width), BF16),
            pltpu.VMEM((width, 2 * width), BF16),
            pltpu.VMEM((width, 2 * width), BF16),
            pltpu.VMEM((size, width), F32),
            pltpu.VMEM((size, width), F32),
            pltpu.VMEM((RELAYED * cols, width), F32),
            pltpu.VMEM((5, 8, width), jnp.int32),
            dma((2,)),
            dma((chunks,)),
            dma((chunks,)),
            dma((chunks,)),
            dma((chunks,)),
            dma((chunks,)),
            dma((chunks,)),
            dma((chunks,)),
            dma((chunks,)),
            dma((chunks,)),
            dma((6,)),
            dma((5,)),
            dma((5,)),
            pltpu.SemaphoreType.REGULAR,
        ],
        compiler_params=pltpu.CompilerParams(
            collective_id=0, has_side_effects=True, vmem_limit_bytes=48 * 2**20
        ),
    )(residual, small)


def solution(mesh):
    in_specs = (P("pix", None, "mz"), P("pix", None), P("mz"), P(), P())
    out_specs = P("pix", None, "mz")
    return jax.shard_map(
        per_device, mesh=mesh, in_specs=in_specs, out_specs=out_specs, check_vma=False
    )
```
